1024 devices in a mesh: node: 16 (over z), local: 64 (over y, x, core).
Axes of the slice: x: 4, y: 8, z: 16, core: 2. Of those that a mesh axis runs over, the one named last changes fastest.
Arguments:
- tokens: bfloat16 [1024, 3584], P(('node', 'local')), may hold values from -6 to 6
- out_grad: bfloat16 [1024, 3584], P(('node', 'local')), may hold values from -2 to 2
- gate_prob: bfloat16 [1024, 8], P(('node', 'local')), may hold values from 0.099609375 to 1
- dest_node: int32 [1024, 8], P(('node', 'local')), may hold values from 0 to 15, as said below
- w_gate: bfloat16 [1024, 3584, 128], P(('node', 'local')), may hold values from -0.09375 to 0.09375
- w_up: bfloat16 [1024, 3584, 128], P(('node', 'local')), may hold values from -0.09375 to 0.09375
- w_down: bfloat16 [1024, 128, 3584], P(('node', 'local')), may hold values from -0.1875 to 0.1875
Outputs:
- in_grad: bfloat16 [1024, 3584], P(('node', 'local'))
- gate_grad: float32 [1024, 8], P(('node', 'local'))
The draws below stay inside these ranges and needn't reach their ends.
Inputs may be any that keep to these rules, and one draw needn't show every extreme that they name: `dest_node`: columns 2 * g and 2 * g + 1 of a row are equal, so a token names at most half of 8 node groups, two experts in each. Among the 64 tokens of one node group, at most 8 name the same node group in one column; for each pair of columns one node group, the same for all source groups, is named by exactly 8 of them.
All inputs are finite; a program needn't handle non-finite values.
Results may differ from the reference program's by a relative error of at most 0.006.
Values may be sent and summed in bfloat16 or wider, within the bound.
No kernel may reach another device: no remote copies, remote signals or barrier semaphores. Data moves between devices by JAX's collectives and lax.ppermute only.
A program may use at most 32 MiB of HBM per device.

```python
import math
import jax
import jax.numpy as jnp
from jax import lax

D = 3584
FF = 1024
EXP_NODE = 8
TOK_DEV = 1
SHARDS = 8
FF_DEV = 128
CAP = 8
EXPERTS = 128
TOKENS = 1024
N_NODE = 16
N_LOCAL = 64


def draw_dest_node(key, part):
    key = jax.random.fold_in(key, 7)
    members = N_LOCAL * TOK_DEV
    pairs = EXP_NODE // 2
    capacity = 2 * members // N_NODE
    key_busy, key_perm = jax.random.split(key)
    busy = jax.random.randint(key_busy, (1, pairs, 1), 0, N_NODE)
    perm_keys = jax.random.split(key_perm, N_NODE * pairs)
    ranks = jax.vmap(partial_permutation(members))(perm_keys).reshape(N_NODE, pairs, members)
    spill = jnp.maximum(ranks - capacity, 0) % max(N_NODE - 1, 1)
    others = (busy + 1 + spill) % N_NODE
    chosen = jnp.where(ranks < capacity, busy, others)
    chosen = jnp.repeat(chosen, 2, axis=1)
    return chosen.transpose(0, 2, 1).reshape(N_NODE * members, EXP_NODE).astype(jnp.int32)


def partial_permutation(members):

    def permute(single_key):
        return jax.random.permutation(single_key, members)
    return permute


def block_levels(stream_key, dims, cuts, least, high):
    factor_of = 1.0
    for axis_at, blocks in cuts:
        draws = jax.random.uniform(jax.random.fold_in(jax.random.fold_in(stream_key, 6), axis_at), (blocks,), jnp.float32, least / len(cuts), high / len(cuts))
        factor_of = factor_of * jnp.repeat(jnp.exp(draws), dims[axis_at] // blocks).reshape((-1,) + (1,) * (len(dims) - 1 - axis_at))
    return factor_of


def centred(rng, shape, width, bound, pieces=(), kind=jnp.bfloat16):
    drawn = jax.random.normal(rng, shape, jnp.float32) * width
    if len(pieces) > 0:
        drawn = block_levels(rng, shape, pieces, -0.22, 0.18) * drawn
    return jnp.clip(drawn, min=-bound, max=bound).astype(kind)


def setup_inputs(seed: int = 0) -> dict:
    arg_keys = jax.random.split(jax.random.key(seed), 8)
    tokens = centred(arg_keys[0], (TOKENS, D), 1.0, 6.0, ((0, 1024),))
    out_grad = centred(arg_keys[1], (TOKENS, D), 0.3, 2.0, ((0, 1024),))
    gate_prob = jnp.clip(jnp.exp(math.log(1.0) - 2.306499 * jax.random.uniform(arg_keys[2], (TOKENS, EXP_NODE), jnp.float32) ** block_levels(arg_keys[2], (TOKENS, EXP_NODE), ((0, 1024),), -0.2, 0.2)), 0.099609375, 1.0).astype(jnp.bfloat16)
    dest_node = draw_dest_node(jax.random.fold_in(arg_keys[7], 71), 0)
    w_gate = centred(arg_keys[4], (EXPERTS * SHARDS, D, FF_DEV), D ** -0.5, 0.09375, ((0, 1024),))
    w_up = centred(arg_keys[5], (EXPERTS * SHARDS, D, FF_DEV), D ** -0.5, 0.09375, ((0, 1024),))
    w_down = centred(arg_keys[6], (EXPERTS * SHARDS, FF_DEV, D), FF ** -0.5, 0.1875, ((0, 1024),))
    return dict(tokens=tokens, out_grad=out_grad, gate_prob=gate_prob, dest_node=dest_node, w_gate=w_gate, w_up=w_up, w_down=w_down)


def expert_terms(rows_x, rows_dy, rows_gate, weight_gate, weight_up, weight_down):
    contract = (((1,), (1,)), ((), ()))
    pre_gate = jnp.dot(rows_x, weight_gate, preferred_element_type=jnp.float32)
    pre_up = jnp.dot(rows_x, weight_up, preferred_element_type=jnp.float32)
    logistic = jax.nn.sigmoid(pre_gate)
    swished = pre_gate * logistic
    hidden = swished * pre_up
    back_hidden = lax.dot_general(rows_dy, weight_down, contract, preferred_element_type=jnp.float32)
    gate_terms = jnp.sum(hidden * back_hidden, axis=1)
    scaled = rows_gate[:, None] * back_hidden
    grad_gate = (scaled * pre_up * logistic * (1.0 + pre_gate * (1.0 - logistic))).astype(jnp.bfloat16)
    grad_up = (scaled * swished).astype(jnp.bfloat16)
    input_terms = lax.dot_general(grad_gate, weight_gate, contract, preferred_element_type=jnp.float32)
    input_terms = input_terms + lax.dot_general(grad_up, weight_up, contract, preferred_element_type=jnp.float32)
    return input_terms, gate_terms


def reference(tokens, out_grad, gate_prob, dest_node, w_gate, w_up, w_down):
    experts = N_NODE * EXP_NODE
    limit = N_NODE * CAP
    full_gate = w_gate.reshape(experts, SHARDS, D, FF_DEV).transpose(0, 2, 1, 3).reshape(experts, D, FF)
    full_up = w_up.reshape(experts, SHARDS, D, FF_DEV).transpose(0, 2, 1, 3).reshape(experts, D, FF)
    full_down = w_down.reshape(experts, FF, D)
    pad_x = jnp.concatenate([tokens, jnp.zeros((1, D), tokens.dtype)], 0)
    pad_dy = jnp.concatenate([out_grad, jnp.zeros((1, D), out_grad.dtype)], 0)
    pad_gate = jnp.concatenate([gate_prob.astype(jnp.float32), jnp.zeros((1, EXP_NODE), jnp.float32)], 0)

    def add_expert(expert, carry):
        acc_x, acc_gate = carry
        column = expert % EXP_NODE
        group_id = expert // EXP_NODE
        chosen = jnp.take(dest_node, column, axis=1) == group_id
        index = jnp.nonzero(chosen, size=limit, fill_value=TOKENS)[0].astype(jnp.int32)
        rows_gate = jnp.take(jnp.take(pad_gate, column, axis=1), index)
        input_terms, gate_terms = expert_terms(pad_x[index], pad_dy[index], rows_gate,
                                               full_gate[expert], full_up[expert], full_down[expert])
        acc_x = acc_x.at[index].add(input_terms)
        onehot = (jnp.arange(EXP_NODE) == column).astype(acc_gate.dtype)
        acc_gate = acc_gate.at[index].add(gate_terms[:, None] * onehot[None, :])
        return acc_x, acc_gate

    start = (jnp.zeros((TOKENS + 1, D), jnp.float32), jnp.zeros((TOKENS + 1, EXP_NODE), jnp.float32))
    acc_x, acc_gate = lax.fori_loop(0, experts, add_expert, start)
    return acc_x[:TOKENS].astype(jnp.bfloat16), acc_gate[:TOKENS]
```

```python
import jax
import jax.numpy as jnp
from jax import lax
from jax.experimental import pallas as pl
from jax.experimental.pallas import tpu as pltpu
from jax.sharding import Mesh
from jax.sharding import PartitionSpec as P

AXES = ("z", "yh", "yl", "x", "c")
LOCAL = ("yh", "yl", "x", "c")
QUAD = ("yl", "x")
F32 = jnp.float32
BF16 = jnp.bfloat16
LANES = 128
SLOTS = 8
NT = (((1,), (1,)), ((), ()))
TN = (((0,), (0,)), ((), ()))


def dot(a, b, dims=(((1,), (0,)), ((), ()))):
    return lax.dot_general(a, b, dims, preferred_element_type=F32)


def exchange(value, axes):
    return lax.all_to_all(value, axes, split_axis=0, concat_axis=0, tiled=True)


def place_kernel(where_ref, got_ref, send_ref, place_ref, wide):
    tokens, slots = place_ref.shape
    wide[...] = got_ref[...].astype(F32)
    aux = wide[pl.ds(4, tokens, stride=8), :]
    lane = lax.broadcasted_iota(jnp.int32, (tokens, LANES), 1)
    pair = where_ref[0]
    dest = jnp.sum(jnp.where(lane == 8 + 2 * pair, aux, 0.0), axis=1, keepdims=True)
    named = (dest == lane.astype(F32)).astype(F32)
    row = lax.broadcasted_iota(jnp.int32, (tokens, tokens), 0)
    col = lax.broadcasted_iota(jnp.int32, (tokens, tokens), 1)
    earlier = (col < row).astype(F32).astype(BF16)
    before = dot(earlier, named.astype(BF16))
    rank = jnp.sum(before * named, axis=1, keepdims=True)
    code = dest * SLOTS + rank
    slot = lax.broadcasted_iota(jnp.int32, (tokens, slots), 1).astype(F32)
    place = (code == slot).astype(F32).astype(BF16)
    place_ref[...] = place
    for k in range(4):
        part = wide[pl.ds(k, tokens, stride=8), :].astype(BF16)
        send_ref[:, k * LANES : (k + 1) * LANES] = dot(place, part, TN).astype(BF16)


def place_rows(where, got, slots):
    tokens = got.shape[0]
    return pl.pallas_call(
        place_kernel,
        out_shape=(
            jax.ShapeDtypeStruct((slots, 4 * LANES), BF16),
            jax.ShapeDtypeStruct((tokens, slots), BF16),
        ),
        in_specs=[
            pl.BlockSpec(memory_space=pltpu.SMEM),
            pl.BlockSpec(memory_space=pltpu.VMEM),
        ],
        out_specs=(
            pl.BlockSpec(memory_space=pltpu.VMEM),
            pl.BlockSpec(memory_space=pltpu.VMEM),
        ),
        scratch_shapes=[pltpu.VMEM((tokens * 8, LANES), F32)],
    )(where, got.reshape(tokens * 8, LANES))


def expert_kernel(where_ref, own_ref, oth_ref, wg_ref, wu_ref, wd_ref, keep_ref, give_ref):
    column, core = where_ref[1], where_ref[2]
    rows = own_ref.shape[1]
    gate = jnp.zeros((rows, LANES), F32)
    up = jnp.zeros((rows, LANES), F32)
    back = jnp.zeros((rows, LANES), F32)
    half = 3 * LANES

    def last_tile(q):
        mine = own_ref[q, :, half:]
        other = oth_ref[q, :, half:]
        return jnp.where(core == 0, mine, other), jnp.where(core == 0, other, mine)

    for i in range(4):
        base = 7 * LANES * i
        lo = pl.multiple_of(base + half * core, LANES)
        hi = pl.multiple_of(base + half * (1 - core), LANES)
        tail, _ = last_tile(i)
        for at, width, v in (
            (lo, half, own_ref[i, :, :half]),
            (hi, half, oth_ref[i, :, :half]),
            (base + 2 * half, LANES, tail),
        ):
            gate += dot(v, wg_ref[pl.ds(at, width), :])
            up += dot(v, wu_ref[pl.ds(at, width), :])
        tail, _ = last_tile(4 + i)
        for at, width, v in (
            (lo, half, own_ref[4 + i, :, :half]),
            (hi, half, oth_ref[4 + i, :, :half]),
            (base + 2 * half, LANES, tail),
        ):
            back += dot(v, wd_ref[:, pl.ds(at, width)], NT)

    _, aux = last_tile(0)
    lane = lax.broadcasted_iota(jnp.int32, (rows, LANES), 1)
    prob = jnp.sum(jnp.where(lane == column, aux.astype(F32), 0.0), axis=1, keepdims=True)
    logistic = jax.nn.sigmoid(gate)
    swished = gate * logistic
    gate_terms = jnp.sum(swished * up * back, axis=1, keepdims=True)
    scaled = prob * back
    grad_gate = (scaled * up * logistic * (1.0 + gate * (1.0 - logistic))).astype(BF16)
    grad_up = (scaled * swished).astype(BF16)
    width = keep_ref.shape[2]
    for ref, side in ((give_ref, 1 - core), (keep_ref, core)):
        for q in range(7):
            at = pl.ds(pl.multiple_of(2 * width * q + width * side, width), width)
            terms = dot(grad_gate, wg_ref[at, :], NT) + dot(grad_up, wu_ref[at, :], NT)
            ref[q] = terms.astype(ref.dtype)
        wide = lax.broadcasted_iota(jnp.int32, (rows, width), 1)
        here = jnp.logical_and(wide == column, side == 0)
        ref[7] = jnp.where(here, gate_terms, 0.0).astype(ref.dtype)


def expert_terms(where, own, oth, wg, wu, wd):
    rows = own.shape[1]
    return pl.pallas_call(
        expert_kernel,
        out_shape=(
            jax.ShapeDtypeStruct((8, rows, 2 * LANES), F32),
            jax.ShapeDtypeStruct((8, rows, 2 * LANES), BF16),
        ),
        in_specs=[pl.BlockSpec(memory_space=pltpu.SMEM)]
        + [pl.BlockSpec(memory_space=pltpu.VMEM)] * 5,
        out_specs=(
            pl.BlockSpec(memory_space=pltpu.VMEM),
            pl.BlockSpec(memory_space=pltpu.VMEM),
        ),
        compiler_params=pltpu.CompilerParams(vmem_limit_bytes=32 * 1024 * 1024),
        cost_estimate=pl.CostEstimate(
            flops=10 * rows * 3584 * LANES, bytes_accessed=6 << 20, transcendentals=rows * LANES
        ),
    )(where, own, oth, wg, wu, wd)


def on_device(tokens, out_grad, gate_prob, dest_node, w_gate, w_up, w_down):
    nodes = lax.axis_size("z")
    width = tokens.shape[1]
    slots = nodes * SLOTS
    pair = lax.axis_index("yh")
    core = lax.axis_index("c")
    where = jnp.stack([pair, 2 * pair + lax.axis_index("yl"), core]).astype(jnp.int32)

    pieces = jnp.concatenate(
        [tokens.reshape(4, 7, LANES), out_grad.reshape(4, 7, LANES)], axis=0
    )
    aux = jnp.concatenate([gate_prob[0], dest_node[0].astype(BF16)])
    aux = jnp.broadcast_to(jnp.pad(aux, (0, LANES - 16)), (8, 1, LANES))
    first = jnp.concatenate([pieces[:, :3], pieces[:, 6:7], aux], axis=1)
    second = jnp.concatenate([pieces[:, 3:6], aux, aux], axis=1)
    both = jnp.pad(jnp.stack([first, second], axis=1), ((0, 0), (0, 0), (0, 3), (0, 0)))
    out = jnp.broadcast_to(both.reshape(1, 16, 8, LANES), (4, 16, 8, LANES))
    got = exchange(out.reshape(64, 8, LANES), LOCAL)

    send, place = place_rows(where, got, 16 * SLOTS)
    send = send[:slots]
    rows = exchange(send.reshape(nodes, SLOTS, 4 * LANES), "z").reshape(slots, 4 * LANES)

    own = exchange(jnp.broadcast_to(rows[None], (8, slots, 4 * LANES)), QUAD)
    swap = ((0, 1), (1, 0))
    oth = lax.ppermute(own, "c", swap)
    keep, give = expert_terms(where, own, oth, w_gate[0], w_up[0], w_down[0])

    took = lax.ppermute(give, "c", swap)
    terms = exchange((keep + took.astype(F32)).astype(BF16), QUAD)
    summed = jnp.sum(terms.astype(F32), axis=0).astype(BF16)

    back = exchange(summed.reshape(nodes, SLOTS, 2 * LANES), "z").reshape(slots, 2 * LANES)
    chosen = dot(place[:, :slots], back).astype(BF16)
    home = exchange(chosen.reshape(64, 2, LANES), LOCAL)
    total = jnp.sum(home.reshape(4, 16, 2 * LANES).astype(F32), axis=0)
    in_grad = total[: width // (2 * LANES)].reshape(1, width).astype(BF16)
    return in_grad, total[14:15, :8]


def solution(mesh):
    fine = Mesh(mesh.devices.reshape(mesh.devices.shape[0], 4, 2, 4, 2), AXES)
    row = P(AXES, None)
    block = P(AXES, None, None)
    return jax.shard_map(
        on_device,
        mesh=fine,
        in_specs=(row, row, row, row, block, block, block),
        out_specs=(row, row),
        check_vma=False,
    )
```

```python
import jax
import jax.numpy as jnp
from jax import lax
from jax.experimental import pallas as pl
from jax.experimental.pallas import tpu as pltpu
from jax.sharding import Mesh
from jax.sharding import PartitionSpec as P

AXES = ("z", "yh", "yl", "x", "c")
LOCAL = ("yh", "yl", "x", "c")
QUAD = ("yl", "x")
SWAP = ((0, 1), (1, 0))
F32 = jnp.float32
BF16 = jnp.bfloat16
LANES = 128
TILES = 7
PIECE = TILES * LANES
HALF = 4
BACK = 512
NT = (((1,), (1,)), ((), ()))
TN = (((0,), (0,)), ((), ()))
VMEM = pl.BlockSpec(memory_space=pltpu.VMEM)
HBM = pl.BlockSpec(memory_space=pltpu.HBM)
WHOLE = 56
MOST = 51
MIB = 1024 * 1024


def dot(a, b, dims=(((1,), (0,)), ((), ()))):
    return lax.dot_general(a, b, dims, preferred_element_type=F32)


def exchange(value, axes):
    return lax.all_to_all(value, axes, split_axis=0, concat_axis=0, tiled=True)


def pack_kernel(x_hbm, dy_hbm, gate_hbm, dest_hbm, out_ref, x_ref, dy_ref, gate_ref, dest_ref, arrived):
    copies = [
        pltpu.make_async_copy(source, target, arrived.at[i])
        for i, (source, target) in enumerate(
            ((x_hbm, x_ref), (dy_hbm, dy_ref), (gate_hbm, gate_ref), (dest_hbm, dest_ref))
        )
    ]
    for copy in copies:
        copy.start()
    for copy in copies:
        copy.wait()
    gate = gate_ref[...].astype(F32)
    dest = dest_ref[...].astype(F32)
    aux = jnp.concatenate([gate, dest, jnp.zeros((1, LANES - 16), F32)], axis=1)
    for q in range(8):
        ref, base = (x_ref, q * PIECE) if q < 4 else (dy_ref, (q - 4) * PIECE)
        rows = [ref[:, base + k * LANES : base + (k + 1) * LANES].astype(F32) for k in range(TILES)]
        tile = jnp.concatenate(rows + [aux], axis=0).astype(BF16)
        for pair in range(4):
            for core in range(2):
                out_ref[pair * 16 + q * 2 + core] = tile


def place_kernel(got_ref, send_ref, place_ref, wide):
    tokens, slots = place_ref.shape
    pair = lax.axis_index("yh")
    core = lax.axis_index("c")
    wide[...] = got_ref[...].astype(F32)
    aux = wide[pl.ds(TILES, tokens, stride=8), :]
    lane = lax.broadcasted_iota(jnp.int32, (tokens, LANES), 1)
    dest = jnp.sum(jnp.where(lane == 8 + 2 * pair, aux, 0.0), axis=1, keepdims=True)
    named = (dest == lane.astype(F32)).astype(F32)
    row = lax.broadcasted_iota(jnp.int32, (tokens, tokens), 0)
    col = lax.broadcasted_iota(jnp.int32, (tokens, tokens), 1)
    earlier = (col < row).astype(F32).astype(BF16)
    before = dot(earlier, named.astype(BF16))
    rank = jnp.sum(before * named, axis=1, keepdims=True)
    slot = lax.broadcasted_iota(jnp.int32, (tokens, slots), 1).astype(F32)
    at = rank - HALF * core.astype(F32)
    code = jnp.where(jnp.logical_and(at >= 0.0, at < HALF), dest * HALF + at, -1.0)
    place = (code == slot).astype(F32).astype(BF16)
    place_ref[...] = place
    for k in range(TILES + 1):
        part = wide[pl.ds(k, tokens, stride=8), :].astype(BF16)
        send_ref[:, k * LANES : (k + 1) * LANES] = dot(place, part, TN).astype(BF16)


def expert_kernel(aux_ref, rows_ref, *refs):
    sources, (out_ref, *weights, arrived) = refs[:6], refs[6:]
    copies = [
        pltpu.make_async_copy(source, target, arrived.at[i])
        for i, (source, target) in enumerate(zip(sources, weights))
    ]
    for copy in copies:
        copy.start()
    column = 2 * lax.axis_index("yh") + lax.axis_index("yl")
    rows = rows_ref.shape[1]
    lane = lax.broadcasted_iota(jnp.int32, (rows, LANES), 1)
    prob = jnp.where(lane == column, aux_ref[...].astype(F32), 0.0)
    prob = jnp.sum(prob, axis=1, keepdims=True)
    gate_terms = jnp.zeros((rows, 1), F32)
    grads = []
    for core in range(2):
        gate_w, up_w, down_w = weights[3 * core : 3 * core + 3]
        for copy in copies[3 * core : 3 * core + 3]:
            copy.wait()
        gate = jnp.zeros((rows, LANES), F32)
        up = jnp.zeros((rows, LANES), F32)
        back = jnp.zeros((rows, LANES), F32)
        for i in range(4):
            at = slice(i * PIECE, (i + 1) * PIECE)
            gate += dot(rows_ref[i], gate_w[at, :])
            up += dot(rows_ref[i], up_w[at, :])
            back += dot(rows_ref[4 + i], down_w[:, at], NT)
        logistic = jax.nn.sigmoid(gate)
        swished = gate * logistic
        gate_terms += jnp.sum(swished * up * back, axis=1, keepdims=True)
        scaled = prob * back
        slope = scaled * up * logistic * (1.0 + gate * (1.0 - logistic))
        grads += [(slope.astype(BF16), gate_w), ((scaled * swished).astype(BF16), up_w)]
    for q in range(7):
        at = slice(q * BACK, (q + 1) * BACK)
        terms = sum(dot(grad, weight[at, :], NT) for grad, weight in grads)
        out_ref[q] = terms.astype(BF16)
    wide = lax.broadcasted_iota(jnp.int32, (rows, BACK), 1)
    out_ref[7] = jnp.where(wide == column, gate_terms, 0.0).astype(BF16)


def on_device(tokens, out_grad, gate_prob, dest_node, w_gate, w_up, w_down):
    nodes = lax.axis_size("z")
    width = tokens.shape[1]
    slots = nodes * HALF
    weights = (w_gate[0], w_up[0], w_down[0])

    out = pl.pallas_call(
        pack_kernel,
        out_shape=jax.ShapeDtypeStruct((64, 8, LANES), BF16),
        in_specs=[HBM] * 4,
        out_specs=VMEM,
        scratch_shapes=[
            pltpu.VMEM(tokens.shape, BF16),
            pltpu.VMEM(out_grad.shape, BF16),
            pltpu.VMEM(gate_prob.shape, BF16),
            pltpu.VMEM(dest_node.shape, jnp.int32),
            pltpu.SemaphoreType.DMA((4,)),
        ],
        compiler_params=pltpu.CompilerParams(vmem_limit_bytes=WHOLE * MIB),
    )(tokens, out_grad, gate_prob, dest_node)
    got = exchange(out, LOCAL)

    send, place = pl.pallas_call(
        place_kernel,
        out_shape=(
            jax.ShapeDtypeStruct((16 * HALF, PIECE + LANES), BF16),
            jax.ShapeDtypeStruct((64, 16 * HALF), BF16),
        ),
        in_specs=[VMEM],
        out_specs=(VMEM, VMEM),
        scratch_shapes=[pltpu.VMEM((64 * 8, LANES), F32)],
        compiler_params=pltpu.CompilerParams(vmem_limit_bytes=4 * MIB),
    )(got.reshape(64 * 8, LANES))
    rows = exchange(send[:slots].reshape(nodes, HALF, PIECE + LANES), "z")
    rows = rows.reshape(slots, PIECE + LANES)

    others = [lax.ppermute(weight, "c", SWAP) for weight in weights]
    own = exchange(jnp.broadcast_to(rows[None, :, :PIECE], (8, slots, PIECE)), QUAD)
    partial = pl.pallas_call(
        expert_kernel,
        out_shape=jax.ShapeDtypeStruct((8, slots, BACK), BF16),
        in_specs=[VMEM] * 2 + [HBM] * 6,
        out_specs=VMEM,
        scratch_shapes=[
            *[pltpu.VMEM(weight.shape, BF16) for weight in (*weights, *weights)],
            pltpu.SemaphoreType.DMA((6,)),
        ],
        compiler_params=pltpu.CompilerParams(vmem_limit_bytes=MOST * MIB),
        cost_estimate=pl.CostEstimate(
            flops=20 * slots * width * LANES,
            bytes_accessed=8 * MIB,
            transcendentals=2 * slots * LANES,
        ),
    )(rows[:, PIECE:], own, *weights, *others)

    terms = exchange(partial, QUAD)
    summed = jnp.sum(terms.astype(F32), axis=0).astype(BF16)

    back = exchange(summed.reshape(nodes, HALF, BACK), "z").reshape(slots, BACK)
    chosen = dot(place[:, :slots], back).astype(BF16)
    home = exchange(chosen.reshape(64, BACK // LANES, LANES), LOCAL)
    total = jnp.sum(home.reshape(4, 8, 2, BACK).astype(F32), axis=(0, 2))
    return total[:7].reshape(1, width).astype(BF16), total[7:, :8]


def solution(mesh):
    fine = Mesh(mesh.devices.reshape(mesh.devices.shape[0], 4, 2, 4, 2), AXES)
    row = P(AXES, None)
    block = P(AXES, None, None)
    return jax.shard_map(
        on_device,
        mesh=fine,
        in_specs=(row, row, row, row, block, block, block),
        out_specs=(row, row),
        check_vma=False,
    )
```

```python
import jax
import jax.numpy as jnp
from jax import lax
from jax.experimental import pallas as pl
from jax.experimental.pallas import tpu as pltpu
from jax.sharding import Mesh
from jax.sharding import PartitionSpec as P

AXES = ("z", "yh", "yl", "x", "c")
LOCAL = ("yh", "yl", "x", "c")
QUAD = ("yl", "x")
SWAP = ((0, 1), (1, 0))
F32 = jnp.float32
BF16 = jnp.bfloat16
LANES = 128
TILES = 7
PIECE = TILES * LANES
HALF = 4
BACK = 512
NT = (((1,), (1,)), ((), ()))
TN = (((0,), (0,)), ((), ()))
VMEM = pl.BlockSpec(memory_space=pltpu.VMEM)
HBM = pl.BlockSpec(memory_space=pltpu.HBM)
WHOLE = 56
MIB = 1024 * 1024


def dot(a, b, dims=(((1,), (0,)), ((), ()))):
    return lax.dot_general(a, b, dims, preferred_element_type=F32)


def exchange(value, axes):
    return lax.all_to_all(value, axes, split_axis=0, concat_axis=0, tiled=True)


def pack_kernel(x_hbm, dy_hbm, gate_hbm, dest_hbm, out_ref, x_ref, dy_ref, gate_ref, dest_ref, arrived):
    copies = [
        pltpu.make_async_copy(source, target, arrived.at[i])
        for i, (source, target) in enumerate(
            ((x_hbm, x_ref), (dy_hbm, dy_ref), (gate_hbm, gate_ref), (dest_hbm, dest_ref))
        )
    ]
    for copy in copies:
        copy.start()
    for copy in copies:
        copy.wait()
    gate = gate_ref[...].astype(F32)
    dest = dest_ref[...].astype(F32)
    aux = jnp.concatenate([gate, dest, jnp.zeros((1, LANES - 16), F32)], axis=1)
    for q in range(8):
        ref, base = (x_ref, q * PIECE) if q < 4 else (dy_ref, (q - 4) * PIECE)
        rows = [ref[:, base + k * LANES : base + (k + 1) * LANES].astype(F32) for k in range(TILES)]
        tile = jnp.concatenate(rows + [aux], axis=0).astype(BF16)
        for pair in range(4):
            for core in range(2):
                out_ref[pair * 16 + q * 2 + core] = tile


def place_kernel(got_ref, send_ref, place_ref, wide):
    tokens, slots = place_ref.shape
    pair = lax.axis_index("yh")
    core = lax.axis_index("c")
    wide[...] = got_ref[...].astype(F32)
    aux = wide[pl.ds(TILES, tokens, stride=8), :]
    lane = lax.broadcasted_iota(jnp.int32, (tokens, LANES), 1)
    dest = jnp.sum(jnp.where(lane == 8 + 2 * pair, aux, 0.0), axis=1, keepdims=True)
    named = (dest == lane.astype(F32)).astype(F32)
    row = lax.broadcasted_iota(jnp.int32, (tokens, tokens), 0)
    col = lax.broadcasted_iota(jnp.int32, (tokens, tokens), 1)
    earlier = (col < row).astype(F32).astype(BF16)
    before = dot(earlier, named.astype(BF16))
    rank = jnp.sum(before * named, axis=1, keepdims=True)
    slot = lax.broadcasted_iota(jnp.int32, (tokens, slots), 1).astype(F32)
    at = rank - HALF * core.astype(F32)
    code = jnp.where(jnp.logical_and(at >= 0.0, at < HALF), dest * HALF + at, -1.0)
    place = (code == slot).astype(F32).astype(BF16)
    place_ref[...] = place
    for k in range(TILES + 1):
        part = wide[pl.ds(k, tokens, stride=8), :].astype(BF16)
        send_ref[:, k * LANES : (k + 1) * LANES] = dot(place, part, TN).astype(BF16)


def expert_kernel(aux_ref, rows_ref, wg_ref, wu_ref, wd_ref, *refs):
    sources, (out_ref, *others, arrived) = refs[:3], refs[3:]
    copies = [
        pltpu.make_async_copy(source, target, arrived.at[i])
        for i, (source, target) in enumerate(zip(sources, others))
    ]
    for copy in copies:
        copy.start()
    column = 2 * lax.axis_index("yh") + lax.axis_index("yl")
    rows = rows_ref.shape[1]
    lane = lax.broadcasted_iota(jnp.int32, (rows, LANES), 1)
    prob = jnp.where(lane == column, aux_ref[...].astype(F32), 0.0)
    prob = jnp.sum(prob, axis=1, keepdims=True)
    gate_terms = jnp.zeros((rows, 1), F32)
    grads = []
    for core, (gate_w, up_w, down_w) in enumerate(((wg_ref, wu_ref, wd_ref), others)):
        if core == 1:
            copies[0].wait()
            copies[1].wait()
        both = dot(rows_ref[0], jnp.concatenate([gate_w[...], up_w[...]], axis=1))
        gate, up = both[:, :LANES], both[:, LANES:]
        if core == 1:
            copies[2].wait()
        back = dot(rows_ref[1], down_w[...], NT)
        logistic = jax.nn.sigmoid(gate)
        swished = gate * logistic
        gate_terms += jnp.sum(swished * up * back, axis=1, keepdims=True)
        scaled = prob * back
        slope = scaled * up * logistic * (1.0 + gate * (1.0 - logistic))
        grads += [slope.astype(BF16), (scaled * swished).astype(BF16)]
    grad = jnp.concatenate(grads, axis=1)
    for q in range(7):
        at = slice(q * BACK, (q + 1) * BACK)
        weight = [ref[at, :] for ref in (wg_ref, wu_ref, others[0], others[1])]
        out_ref[q] = dot(grad, jnp.concatenate(weight, axis=1), NT).astype(BF16)
    wide = lax.broadcasted_iota(jnp.int32, (rows, BACK), 1)
    out_ref[7] = jnp.where(wide == column, gate_terms, 0.0).astype(BF16)


def on_device(tokens, out_grad, gate_prob, dest_node, w_gate, w_up, w_down):
    nodes = lax.axis_size("z")
    width = tokens.shape[1]
    slots = nodes * HALF
    weights = (w_gate[0], w_up[0], w_down[0])

    out = pl.pallas_call(
        pack_kernel,
        out_shape=jax.ShapeDtypeStruct((64, 8, LANES), BF16),
        in_specs=[HBM] * 4,
        out_specs=VMEM,
        scratch_shapes=[
            pltpu.VMEM(tokens.shape, BF16),
            pltpu.VMEM(out_grad.shape, BF16),
            pltpu.VMEM(gate_prob.shape, BF16),
            pltpu.VMEM(dest_node.shape, jnp.int32),
            pltpu.SemaphoreType.DMA((4,)),
        ],
        compiler_params=pltpu.CompilerParams(vmem_limit_bytes=WHOLE * MIB),
    )(tokens, out_grad, gate_prob, dest_node)
    got = exchange(out, LOCAL)

    send, place = pl.pallas_call(
        place_kernel,
        out_shape=(
            jax.ShapeDtypeStruct((16 * HALF, PIECE + LANES), BF16),
            jax.ShapeDtypeStruct((64, 16 * HALF), BF16),
        ),
        in_specs=[VMEM],
        out_specs=(VMEM, VMEM),
        scratch_shapes=[pltpu.VMEM((64 * 8, LANES), F32)],
        compiler_params=pltpu.CompilerParams(vmem_limit_bytes=4 * MIB),
    )(got.reshape(64 * 8, LANES))
    rows = exchange(send[:slots].reshape(nodes, HALF, PIECE + LANES), "z")
    rows = rows.reshape(slots, PIECE + LANES)

    others = [lax.ppermute(weight, "c", SWAP) for weight in weights]
    own = exchange(jnp.broadcast_to(rows[None, :, :PIECE], (8, slots, PIECE)), QUAD)
    own = own.reshape(2, 4, slots, PIECE).transpose(0, 2, 1, 3).reshape(2, slots, width)
    partial = pl.pallas_call(
        expert_kernel,
        out_shape=jax.ShapeDtypeStruct((8, slots, BACK), BF16),
        in_specs=[VMEM] * 5 + [HBM] * 3,
        out_specs=VMEM,
        scratch_shapes=[
            *[pltpu.VMEM(weight.shape, BF16) for weight in weights],
            pltpu.SemaphoreType.DMA((3,)),
        ],
        compiler_params=pltpu.CompilerParams(vmem_limit_bytes=16 * MIB),
        cost_estimate=pl.CostEstimate(
            flops=20 * slots * width * LANES,
            bytes_accessed=8 * MIB,
            transcendentals=2 * slots * LANES,
        ),
    )(rows[:, PIECE:], own, *weights, *others)

    terms = exchange(partial, QUAD)
    summed = jnp.sum(terms.astype(F32), axis=0).astype(BF16)

    back = exchange(summed.reshape(nodes, HALF, BACK), "z").reshape(slots, BACK)
    chosen = dot(place[:, :slots], back).astype(BF16)
    home = exchange(chosen.reshape(64, BACK // LANES, LANES), LOCAL)
    total = jnp.sum(home.reshape(4, 8, 2, BACK).astype(F32), axis=(0, 2))
    return total[:7].reshape(1, width).astype(BF16), total[7:, :8]


def solution(mesh):
    fine = Mesh(mesh.devices.reshape(mesh.devices.shape[0], 4, 2, 4, 2), AXES)
    row = P(AXES, None)
    block = P(AXES, None, None)
    return jax.shard_map(
        on_device,
        mesh=fine,
        in_specs=(row, row, row, row, block, block, block),
        out_specs=(row, row),
        check_vma=False,
    )
```

```python
import jax
import jax.numpy as jnp
from jax import lax
from jax.experimental import pallas as pl
from jax.experimental.pallas import tpu as pltpu
from jax.sharding import Mesh
from jax.sharding import PartitionSpec as P

AXES = ("z", "yh", "yl", "x", "c")
LOCAL = ("yh", "yl", "x", "c")
QUAD = ("yl", "x")
SWAP = ((0, 1), (1, 0))
F32 = jnp.float32
BF16 = jnp.bfloat16
LANES = 128
TILES = 7
PIECE = TILES * LANES
HALF = 4
BACK = 512
NT = (((1,), (1,)), ((), ()))
TN = (((0,), (0,)), ((), ()))
VMEM = pl.BlockSpec(memory_space=pltpu.VMEM)
HBM = pl.BlockSpec(memory_space=pltpu.HBM)
WHOLE = 56
MIB = 1024 * 1024


def dot(a, b, dims=(((1,), (0,)), ((), ()))):
    return lax.dot_general(a, b, dims, preferred_element_type=F32)


def exchange(value, axes):
    return lax.all_to_all(value, axes, split_axis=0, concat_axis=0, tiled=True)


def pack_kernel(x_hbm, dy_hbm, gate_hbm, dest_hbm, out_ref, x_ref, dy_ref, gate_ref, dest_ref, arrived):
    copies = [
        pltpu.make_async_copy(source, target, arrived.at[i])
        for i, (source, target) in enumerate(
            ((x_hbm, x_ref), (dy_hbm, dy_ref), (gate_hbm, gate_ref), (dest_hbm, dest_ref))
        )
    ]
    for copy in copies:
        copy.start()
    for copy in copies:
        copy.wait()
    gate = gate_ref[...].astype(F32)
    dest = dest_ref[...].astype(F32)
    aux = jnp.concatenate([gate, dest, jnp.zeros((1, LANES - 16), F32)], axis=1)
    for q in range(8):
        ref, base = (x_ref, q * PIECE) if q < 4 else (dy_ref, (q - 4) * PIECE)
        rows = [ref[:, base + k * LANES : base + (k + 1) * LANES].astype(F32) for k in range(TILES)]
        tile = jnp.concatenate(rows + [aux], axis=0).astype(BF16)
        for pair in range(4):
            for core in range(2):
                out_ref[pair * 16 + q * 2 + core] = tile


def weights_kernel(wg_ref, wu_ref, wd_ref, after_ref, out_ref, arrived):
    width = wg_ref.shape[0]
    pairs = [(wg_ref, out_ref.at[:width, :]), (wu_ref, out_ref.at[width : 2 * width, :])]
    for k in range(width // LANES):
        at = slice(k * LANES, (k + 1) * LANES)
        pairs.append((wd_ref.at[:, at], out_ref.at[2 * width + k * LANES : 2 * width + (k + 1) * LANES, :]))
    copies = [
        pltpu.make_async_copy(source, target, arrived.at[i])
        for i, (source, target) in enumerate(pairs)
    ]
    for copy in copies:
        copy.start()
    for copy in copies:
        copy.wait()


def place_kernel(got_ref, send_ref, place_ref, wide):
    tokens, slots = place_ref.shape
    pair = lax.axis_index("yh")
    core = lax.axis_index("c")
    wide[...] = got_ref[...].astype(F32)
    aux = wide[pl.ds(TILES, tokens, stride=8), :]
    lane = lax.broadcasted_iota(jnp.int32, (tokens, LANES), 1)
    dest = jnp.sum(jnp.where(lane == 8 + 2 * pair, aux, 0.0), axis=1, keepdims=True)
    named = (dest == lane.astype(F32)).astype(F32)
    row = lax.broadcasted_iota(jnp.int32, (tokens, tokens), 0)
    col = lax.broadcasted_iota(jnp.int32, (tokens, tokens), 1)
    earlier = (col < row).astype(F32).astype(BF16)
    before = dot(earlier, named.astype(BF16))
    rank = jnp.sum(before * named, axis=1, keepdims=True)
    slot = lax.broadcasted_iota(jnp.int32, (tokens, slots), 1).astype(F32)
    at = rank - HALF * core.astype(F32)
    code = jnp.where(jnp.logical_and(at >= 0.0, at < HALF), dest * HALF + at, -1.0)
    place = (code == slot).astype(F32).astype(BF16)
    place_ref[...] = place
    for k in range(TILES + 1):
        part = wide[pl.ds(k, tokens, stride=8), :].astype(BF16)
        send_ref[:, k * LANES : (k + 1) * LANES] = dot(place, part, TN).astype(BF16)


def expert_kernel(aux_ref, rows_ref, wg_ref, wu_ref, wd_ref, theirs_ref, out_ref, other_ref, arrived):
    copy = pltpu.make_async_copy(theirs_ref, other_ref, arrived)
    copy.start()
    width = wg_ref.shape[0]
    column = 2 * lax.axis_index("yh") + lax.axis_index("yl")
    rows = rows_ref.shape[1]
    lane = lax.broadcasted_iota(jnp.int32, (rows, LANES), 1)
    prob = jnp.where(lane == column, aux_ref[...].astype(F32), 0.0)
    prob = jnp.sum(prob, axis=1, keepdims=True)
    x = jnp.concatenate([rows_ref[i] for i in range(4)], axis=1)
    dy = jnp.concatenate([rows_ref[i] for i in range(4, 8)], axis=1)
    gate_terms = jnp.zeros((rows, 1), F32)
    grads = []
    for core in range(2):
        if core == 0:
            gate_up = jnp.concatenate([wg_ref[...], wu_ref[...]], axis=1)
            down = wd_ref[...]
        else:
            copy.wait()
            gate_up = jnp.concatenate([other_ref[:width, :], other_ref[width : 2 * width, :]], axis=1)
            tiles = range(2 * width, 3 * width, LANES)
            down = jnp.concatenate([other_ref[k : k + LANES, :] for k in tiles], axis=1)
        both = dot(x, gate_up)
        gate, up = both[:, :LANES], both[:, LANES:]
        back = dot(dy, down, NT)
        logistic = jax.nn.sigmoid(gate)
        swished = gate * logistic
        gate_terms += jnp.sum(swished * up * back, axis=1, keepdims=True)
        scaled = prob * back
        slope = scaled * up * logistic * (1.0 + gate * (1.0 - logistic))
        grads += [slope.astype(BF16), (scaled * swished).astype(BF16)]
    grad = jnp.concatenate(grads, axis=1)
    for q in range(7):
        at = slice(q * BACK, (q + 1) * BACK)
        beyond = slice(width + q * BACK, width + (q + 1) * BACK)
        weight = [wg_ref[at, :], wu_ref[at, :], other_ref[at, :], other_ref[beyond, :]]
        out_ref[q] = dot(grad, jnp.concatenate(weight, axis=1), NT).astype(BF16)
    wide = lax.broadcasted_iota(jnp.int32, (rows, BACK), 1)
    out_ref[7] = jnp.where(wide == column, gate_terms, 0.0).astype(BF16)


def on_device(tokens, out_grad, gate_prob, dest_node, w_gate, w_up, w_down):
    nodes = lax.axis_size("z")
    width = tokens.shape[1]
    slots = nodes * HALF
    weights = (w_gate[0], w_up[0], w_down[0])

    out = pl.pallas_call(
        pack_kernel,
        out_shape=jax.ShapeDtypeStruct((64, 8, LANES), BF16),
        in_specs=[HBM] * 4,
        out_specs=VMEM,
        scratch_shapes=[
            pltpu.VMEM(tokens.shape, BF16),
            pltpu.VMEM(out_grad.shape, BF16),
            pltpu.VMEM(gate_prob.shape, BF16),
            pltpu.VMEM(dest_node.shape, jnp.int32),
            pltpu.SemaphoreType.DMA((4,)),
        ],
        compiler_params=pltpu.CompilerParams(vmem_limit_bytes=WHOLE * MIB),
    )(tokens, out_grad, gate_prob, dest_node)
    got = exchange(out, LOCAL)
    packed = pl.pallas_call(
        weights_kernel,
        out_shape=jax.ShapeDtypeStruct((3 * width, LANES), BF16),
        in_specs=[HBM] * 4,
        out_specs=HBM,
        scratch_shapes=[pltpu.SemaphoreType.DMA((2 + width // LANES,))],
        compiler_params=pltpu.CompilerParams(vmem_limit_bytes=WHOLE * MIB),
        cost_estimate=pl.CostEstimate(flops=0, bytes_accessed=6 * MIB, transcendentals=0),
    )(*weights, out)
    got, packed = lax.optimization_barrier((got, packed))
    other = lax.ppermute(packed, "c", SWAP)

    send, place = pl.pallas_call(
        place_kernel,
        out_shape=(
            jax.ShapeDtypeStruct((16 * HALF, PIECE + LANES), BF16),
            jax.ShapeDtypeStruct((64, 16 * HALF), BF16),
        ),
        in_specs=[VMEM],
        out_specs=(VMEM, VMEM),
        scratch_shapes=[pltpu.VMEM((64 * 8, LANES), F32)],
        compiler_params=pltpu.CompilerParams(vmem_limit_bytes=4 * MIB),
    )(got.reshape(64 * 8, LANES))
    rows = exchange(send[:slots].reshape(nodes, HALF, PIECE + LANES), "z")
    rows, other = lax.optimization_barrier((rows.reshape(slots, PIECE + LANES), other))

    aux, spread = rows[:, PIECE:], jnp.broadcast_to(rows[None, :, :PIECE], (8, slots, PIECE))
    aux, spread = lax.optimization_barrier((aux, spread))
    own = exchange(spread, QUAD)
    partial = pl.pallas_call(
        expert_kernel,
        out_shape=jax.ShapeDtypeStruct((8, slots, BACK), BF16),
        in_specs=[VMEM] * 5 + [HBM],
        out_specs=VMEM,
        scratch_shapes=[pltpu.VMEM((3 * width, LANES), BF16), pltpu.SemaphoreType.DMA],
        compiler_params=pltpu.CompilerParams(vmem_limit_bytes=16 * MIB),
        cost_estimate=pl.CostEstimate(
            flops=20 * slots * width * LANES,
            bytes_accessed=8 * MIB,
            transcendentals=2 * slots * LANES,
        ),
    )(aux, own, *weights, other)

    terms = exchange(partial, QUAD)
    summed = jnp.sum(terms.astype(F32), axis=0).astype(BF16)

    back = exchange(summed.reshape(nodes, HALF, BACK), "z").reshape(slots, BACK)
    chosen = dot(place[:, :slots], back).astype(BF16)
    home = exchange(chosen.reshape(64, BACK // LANES, LANES), LOCAL)
    total = jnp.sum(home.reshape(4, 8, 2, BACK).astype(F32), axis=(0, 2))
    return total[:7].reshape(1, width).astype(BF16), total[7:, :8]


def solution(mesh):
    fine = Mesh(mesh.devices.reshape(mesh.devices.shape[0], 4, 2, 4, 2), AXES)
    row = P(AXES, None)
    block = P(AXES, None, None)
    return jax.shard_map(
        on_device,
        mesh=fine,
        in_specs=(row, row, row, row, block, block, block),
        out_specs=(row, row),
        check_vma=False,
    )
```

```python
import jax
import jax.numpy as jnp
from jax import lax
from jax.experimental import pallas as pl
from jax.experimental.pallas import tpu as pltpu
from jax.sharding import Mesh
from jax.sharding import PartitionSpec as P

AXES = ("z", "yh", "yl", "x", "c")
LOCAL = ("yh", "yl", "x", "c")
QUAD = ("yl", "x")
SWAP = ((0, 1), (1, 0))
F32 = jnp.float32
BF16 = jnp.bfloat16
LANES = 128
TILES = 7
PIECE = TILES * LANES
HALF = 4
BACK = 512
NT = (((1,), (1,)), ((), ()))
TN = (((0,), (0,)), ((), ()))
VMEM = pl.BlockSpec(memory_space=pltpu.VMEM)
HBM = pl.BlockSpec(memory_space=pltpu.HBM)
WHOLE = 56
MOST = 51
MIB = 1024 * 1024


def dot(a, b, dims=(((1,), (0,)), ((), ()))):
    return lax.dot_general(a, b, dims, preferred_element_type=F32)


def exchange(value, axes):
    return lax.all_to_all(value, axes, split_axis=0, concat_axis=0, tiled=True)


def pack_kernel(x_hbm, dy_hbm, gate_hbm, dest_hbm, out_ref, x_ref, dy_ref, gate_ref, dest_ref, arrived):
    copies = [
        pltpu.make_async_copy(source, target, arrived.at[i])
        for i, (source, target) in enumerate(
            ((x_hbm, x_ref), (dy_hbm, dy_ref), (gate_hbm, gate_ref), (dest_hbm, dest_ref))
        )
    ]
    for copy in copies:
        copy.start()
    for copy in copies:
        copy.wait()
    gate = gate_ref[...].astype(F32)
    dest = dest_ref[...].astype(F32)
    aux = jnp.concatenate([gate, dest, jnp.zeros((1, LANES - 16), F32)], axis=1)
    for q in range(8):
        ref, base = (x_ref, q * PIECE) if q < 4 else (dy_ref, (q - 4) * PIECE)
        rows = [ref[:, base + k * LANES : base + (k + 1) * LANES].astype(F32) for k in range(TILES)]
        tile = jnp.concatenate(rows + [aux], axis=0).astype(BF16)
        for pair in range(4):
            for core in range(2):
                out_ref[pair * 16 + q * 2 + core] = tile


def place_kernel(got_ref, send_ref, place_ref, wide):
    tokens, slots = place_ref.shape
    pair = lax.axis_index("yh")
    core = lax.axis_index("c")
    wide[...] = got_ref[...].astype(F32)
    aux = wide[pl.ds(TILES, tokens, stride=8), :]
    lane = lax.broadcasted_iota(jnp.int32, (tokens, LANES), 1)
    dest = jnp.sum(jnp.where(lane == 8 + 2 * pair, aux, 0.0), axis=1, keepdims=True)
    named = (dest == lane.astype(F32)).astype(F32)
    row = lax.broadcasted_iota(jnp.int32, (tokens, tokens), 0)
    col = lax.broadcasted_iota(jnp.int32, (tokens, tokens), 1)
    earlier = (col < row).astype(F32).astype(BF16)
    before = dot(earlier, named.astype(BF16))
    rank = jnp.sum(before * named, axis=1, keepdims=True)
    slot = lax.broadcasted_iota(jnp.int32, (tokens, slots), 1).astype(F32)
    at = rank - HALF * core.astype(F32)
    code = jnp.where(jnp.logical_and(at >= 0.0, at < HALF), dest * HALF + at, -1.0)
    place = (code == slot).astype(F32).astype(BF16)
    place_ref[...] = place
    for k in range(TILES + 1):
        part = wide[pl.ds(k, tokens, stride=8), :].astype(BF16)
        send_ref[:, k * LANES : (k + 1) * LANES] = dot(place, part, TN).astype(BF16)


def expert_kernel(aux_ref, rows_ref, *refs):
    sources, (out_ref, *weights, arrived) = refs[:6], refs[6:]
    copies = [
        pltpu.make_async_copy(source, target, arrived.at[i])
        for i, (source, target) in enumerate(zip(sources, weights))
    ]
    for copy in copies:
        copy.start()
    column = 2 * lax.axis_index("yh") + lax.axis_index("yl")
    rows = rows_ref.shape[1]
    lane = lax.broadcasted_iota(jnp.int32, (rows, LANES), 1)
    prob = jnp.where(lane == column, aux_ref[...].astype(F32), 0.0)
    prob = jnp.sum(prob, axis=1, keepdims=True)
    x = jnp.concatenate([rows_ref[i] for i in range(4)], axis=1)
    dy = jnp.concatenate([rows_ref[i] for i in range(4, 8)], axis=1)
    gate_terms = jnp.zeros((rows, 1), F32)
    grads = []
    for core in range(2):
        for copy in copies[3 * core : 3 * core + 3]:
            copy.wait()
        gate_w, up_w, down_w = weights[3 * core : 3 * core + 3]
        both = dot(x, jnp.concatenate([gate_w[...], up_w[...]], axis=1))
        gate, up = both[:, :LANES], both[:, LANES:]
        back = dot(dy, down_w[...], NT)
        logistic = jax.nn.sigmoid(gate)
        swished = gate * logistic
        gate_terms += jnp.sum(swished * up * back, axis=1, keepdims=True)
        scaled = prob * back
        slope = scaled * up * logistic * (1.0 + gate * (1.0 - logistic))
        grads += [slope.astype(BF16), (scaled * swished).astype(BF16)]
    grad = jnp.concatenate(grads, axis=1)
    for q in range(7):
        at = slice(q * BACK, (q + 1) * BACK)
        wide = [weights[i][at, :] for i in (0, 1, 3, 4)]
        out_ref[q] = dot(grad, jnp.concatenate(wide, axis=1), NT).astype(BF16)
    lane = lax.broadcasted_iota(jnp.int32, (rows, BACK), 1)
    out_ref[7] = jnp.where(lane == column, gate_terms, 0.0).astype(BF16)


def sum_kernel(home_ref, grad_ref, gate_ref):
    for q in range(8):
        parts = [home_ref[pair * 16 + q * 2 + core].astype(F32) for pair in range(4) for core in range(2)]
        total = sum(parts)
        if q == 7:
            gate_ref[...] = total[:1, :8]
        else:
            for k in range(BACK // LANES):
                at = q * BACK + k * LANES
                grad_ref[:, at : at + LANES] = total[k : k + 1, :].astype(BF16)


def on_device(tokens, out_grad, gate_prob, dest_node, w_gate, w_up, w_down):
    nodes = lax.axis_size("z")
    width = tokens.shape[1]
    slots = nodes * HALF
    weights = (w_gate[0], w_up[0], w_down[0])

    out = pl.pallas_call(
        pack_kernel,
        out_shape=jax.ShapeDtypeStruct((64, 8, LANES), BF16),
        in_specs=[HBM] * 4,
        out_specs=VMEM,
        scratch_shapes=[
            pltpu.VMEM(tokens.shape, BF16),
            pltpu.VMEM(out_grad.shape, BF16),
            pltpu.VMEM(gate_prob.shape, BF16),
            pltpu.VMEM(dest_node.shape, jnp.int32),
            pltpu.SemaphoreType.DMA((4,)),
        ],
        compiler_params=pltpu.CompilerParams(vmem_limit_bytes=WHOLE * MIB),
    )(tokens, out_grad, gate_prob, dest_node)
    got = exchange(out, LOCAL)

    send, place = pl.pallas_call(
        place_kernel,
        out_shape=(
            jax.ShapeDtypeStruct((16 * HALF, PIECE + LANES), BF16),
            jax.ShapeDtypeStruct((64, 16 * HALF), BF16),
        ),
        in_specs=[VMEM],
        out_specs=(VMEM, VMEM),
        scratch_shapes=[pltpu.VMEM((64 * 8, LANES), F32)],
        compiler_params=pltpu.CompilerParams(vmem_limit_bytes=4 * MIB),
    )(got.reshape(64 * 8, LANES))
    rows = exchange(send[:slots].reshape(nodes, HALF, PIECE + LANES), "z")
    rows = rows.reshape(slots, PIECE + LANES)

    others = [lax.ppermute(weight, "c", SWAP) for weight in weights]
    own = exchange(jnp.broadcast_to(rows[None, :, :PIECE], (8, slots, PIECE)), QUAD)
    partial = pl.pallas_call(
        expert_kernel,
        out_shape=jax.ShapeDtypeStruct((8, slots, BACK), BF16),
        in_specs=[VMEM] * 2 + [HBM] * 6,
        out_specs=VMEM,
        scratch_shapes=[
            *[pltpu.VMEM(weight.shape, BF16) for weight in (*weights, *weights)],
            pltpu.SemaphoreType.DMA((6,)),
        ],
        compiler_params=pltpu.CompilerParams(vmem_limit_bytes=MOST * MIB),
        cost_estimate=pl.CostEstimate(
            flops=20 * slots * width * LANES,
            bytes_accessed=8 * MIB,
            transcendentals=2 * slots * LANES,
        ),
    )(rows[:, PIECE:], own, *weights, *others)

    terms = exchange(partial, QUAD)
    summed = jnp.sum(terms.astype(F32), axis=0).astype(BF16)

    back = exchange(summed.reshape(nodes, HALF, BACK), "z").reshape(slots, BACK)
    chosen = dot(place[:, :slots], back).astype(BF16)
    home = exchange(chosen.reshape(64, BACK // LANES, LANES), LOCAL)
    return pl.pallas_call(
        sum_kernel,
        out_shape=(
            jax.ShapeDtypeStruct((1, width), BF16),
            jax.ShapeDtypeStruct((1, 8), F32),
        ),
        in_specs=[VMEM],
        out_specs=(VMEM, VMEM),
        compiler_params=pltpu.CompilerParams(vmem_limit_bytes=4 * MIB),
    )(home)


def solution(mesh):
    fine = Mesh(mesh.devices.reshape(mesh.devices.shape[0], 4, 2, 4, 2), AXES)
    row = P(AXES, None)
    block = P(AXES, None, None)
    return jax.shard_map(
        on_device,
        mesh=fine,
        in_specs=(row, row, row, row, block, block, block),
        out_specs=(row, row),
        check_vma=False,
    )
```

```python
import jax
import jax.numpy as jnp
from jax import lax
from jax.experimental import pallas as pl
from jax.experimental.pallas import tpu as pltpu
from jax.sharding import Mesh
from jax.sharding import PartitionSpec as P

AXES = ("z", "yh", "yl", "x", "c")
LOCAL = ("yh", "yl", "x", "c")
QUAD = ("yl", "x")
SWAP = ((0, 1), (1, 0))
F32 = jnp.float32
BF16 = jnp.bfloat16
LANES = 128
TILES = 7
PIECE = TILES * LANES
HALF = 4
BACK = 512
NT = (((1,), (1,)), ((), ()))
TN = (((0,), (0,)), ((), ()))
VMEM = pl.BlockSpec(memory_space=pltpu.VMEM)
HBM = pl.BlockSpec(memory_space=pltpu.HBM)
WHOLE = 56
MOST = 51
MIB = 1024 * 1024


def dot(a, b, dims=(((1,), (0,)), ((), ()))):
    return lax.dot_general(a, b, dims, preferred_element_type=F32)


def exchange(value, axes):
    return lax.all_to_all(value, axes, split_axis=0, concat_axis=0, tiled=True)


def pack_kernel(x_hbm, dy_hbm, gate_hbm, dest_hbm, out_ref, x_ref, dy_ref, gate_ref, dest_ref, arrived):
    copies = [
        pltpu.make_async_copy(source, target, arrived.at[i])
        for i, (source, target) in enumerate(
            ((x_hbm, x_ref), (dy_hbm, dy_ref), (gate_hbm, gate_ref), (dest_hbm, dest_ref))
        )
    ]
    for copy in copies:
        copy.start()
    for copy in copies:
        copy.wait()
    gate = gate_ref[...].astype(F32)
    dest = dest_ref[...].astype(F32)
    aux = jnp.concatenate([gate, dest, jnp.zeros((1, LANES - 16), F32)], axis=1)
    for q in range(8):
        ref, base = (x_ref, q * PIECE) if q < 4 else (dy_ref, (q - 4) * PIECE)
        rows = [ref[:, base + k * LANES : base + (k + 1) * LANES].astype(F32) for k in range(TILES)]
        tile = jnp.concatenate(rows + [aux], axis=0).astype(BF16)
        for pair in range(4):
            for core in range(2):
                out_ref[pair * 16 + q * 2 + core] = tile


def place_kernel(got_ref, send_ref, place_ref, wide):
    tokens, slots = place_ref.shape
    pair = lax.axis_index("yh")
    core = lax.axis_index("c")
    wide[...] = got_ref[...].astype(F32)
    aux = wide[pl.ds(TILES, tokens, stride=8), :]
    lane = lax.broadcasted_iota(jnp.int32, (tokens, LANES), 1)
    dest = jnp.sum(jnp.where(lane == 8 + 2 * pair, aux, 0.0), axis=1, keepdims=True)
    named = (dest == lane.astype(F32)).astype(F32)
    row = lax.broadcasted_iota(jnp.int32, (tokens, tokens), 0)
    col = lax.broadcasted_iota(jnp.int32, (tokens, tokens), 1)
    earlier = (col < row).astype(F32).astype(BF16)
    before = dot(earlier, named.astype(BF16))
    rank = jnp.sum(before * named, axis=1, keepdims=True)
    slot = lax.broadcasted_iota(jnp.int32, (tokens, slots), 1).astype(F32)
    at = rank - HALF * core.astype(F32)
    code = jnp.where(jnp.logical_and(at >= 0.0, at < HALF), dest * HALF + at, -1.0)
    place = (code == slot).astype(F32).astype(BF16)
    place_ref[...] = place
    for k in range(TILES + 1):
        part = wide[pl.ds(k, tokens, stride=8), :].astype(BF16)
        send_ref[:, k * LANES : (k + 1) * LANES] = dot(place, part, TN).astype(BF16)


def expert_kernel(aux_ref, rows_ref, *refs):
    sources, (out_ref, *weights, arrived) = refs[:6], refs[6:]
    copies = [
        pltpu.make_async_copy(source, target, arrived.at[i])
        for i, (source, target) in enumerate(zip(sources, weights))
    ]
    for copy in copies:
        copy.start()
    column = 2 * lax.axis_index("yh") + lax.axis_index("yl")
    rows = aux_ref.shape[0]
    lane = lax.broadcasted_iota(jnp.int32, (rows, LANES), 1)
    prob = jnp.where(lane == column, aux_ref[...].astype(F32), 0.0)
    prob = jnp.sum(prob, axis=1, keepdims=True)
    tiles = [
        [rows_ref[q, k * rows : (k + 1) * rows, :] for k in range(TILES)] for q in range(8)
    ]
    x = jnp.concatenate(sum(tiles[:4], []), axis=1)
    dy = jnp.concatenate(sum(tiles[4:], []), axis=1)
    gate_terms = jnp.zeros((rows, 1), F32)
    grads = []
    for core in range(2):
        for copy in copies[3 * core : 3 * core + 3]:
            copy.wait()
        gate_w, up_w, down_w = weights[3 * core : 3 * core + 3]
        both = dot(x, jnp.concatenate([gate_w[...], up_w[...]], axis=1))
        gate, up = both[:, :LANES], both[:, LANES:]
        back = dot(dy, down_w[...], NT)
        logistic = jax.nn.sigmoid(gate)
        swished = gate * logistic
        gate_terms += jnp.sum(swished * up * back, axis=1, keepdims=True)
        scaled = prob * back
        slope = scaled * up * logistic * (1.0 + gate * (1.0 - logistic))
        grads += [slope.astype(BF16), (scaled * swished).astype(BF16)]
    grad = jnp.concatenate(grads, axis=1)
    for q in range(7):
        at = slice(q * BACK, (q + 1) * BACK)
        wide = [weights[i][at, :] for i in (0, 1, 3, 4)]
        out_ref[q] = dot(grad, jnp.concatenate(wide, axis=1), NT).astype(BF16)
    lane = lax.broadcasted_iota(jnp.int32, (rows, BACK), 1)
    out_ref[7] = jnp.where(lane == column, gate_terms, 0.0).astype(BF16)


def sum_kernel(home_ref, grad_ref, gate_ref):
    for q in range(8):
        parts = [home_ref[pair * 16 + q * 2 + core].astype(F32) for pair in range(4) for core in range(2)]
        total = sum(parts)
        if q == 7:
            gate_ref[...] = total[:1, :8]
        else:
            for k in range(BACK // LANES):
                at = q * BACK + k * LANES
                grad_ref[:, at : at + LANES] = total[k : k + 1, :].astype(BF16)


def on_device(tokens, out_grad, gate_prob, dest_node, w_gate, w_up, w_down):
    nodes = lax.axis_size("z")
    width = tokens.shape[1]
    slots = nodes * HALF
    weights = (w_gate[0], w_up[0], w_down[0])

    out = pl.pallas_call(
        pack_kernel,
        out_shape=jax.ShapeDtypeStruct((64, 8, LANES), BF16),
        in_specs=[HBM] * 4,
        out_specs=VMEM,
        scratch_shapes=[
            pltpu.VMEM(tokens.shape, BF16),
            pltpu.VMEM(out_grad.shape, BF16),
            pltpu.VMEM(gate_prob.shape, BF16),
            pltpu.VMEM(dest_node.shape, jnp.int32),
            pltpu.SemaphoreType.DMA((4,)),
        ],
        compiler_params=pltpu.CompilerParams(vmem_limit_bytes=WHOLE * MIB),
    )(tokens, out_grad, gate_prob, dest_node)
    got = exchange(out, LOCAL)

    send, place = pl.pallas_call(
        place_kernel,
        out_shape=(
            jax.ShapeDtypeStruct((16 * HALF, PIECE + LANES), BF16),
            jax.ShapeDtypeStruct((64, 16 * HALF), BF16),
        ),
        in_specs=[VMEM],
        out_specs=(VMEM, VMEM),
        scratch_shapes=[pltpu.VMEM((64 * 8, LANES), F32)],
        compiler_params=pltpu.CompilerParams(vmem_limit_bytes=4 * MIB),
    )(got.reshape(64 * 8, LANES))
    rows = exchange(send[:slots].reshape(nodes, HALF, PIECE + LANES), "z")
    rows = rows.reshape(slots, PIECE + LANES)

    others = [lax.ppermute(weight, "c", SWAP) for weight in weights]
    tiles = rows[:, :PIECE].reshape(slots, TILES, LANES).transpose(1, 0, 2).reshape(TILES * slots, LANES)
    own = exchange(jnp.broadcast_to(tiles[None], (8, TILES * slots, LANES)), QUAD)
    partial = pl.pallas_call(
        expert_kernel,
        out_shape=jax.ShapeDtypeStruct((8, slots, BACK), BF16),
        in_specs=[VMEM] * 2 + [HBM] * 6,
        out_specs=VMEM,
        scratch_shapes=[
            *[pltpu.VMEM(weight.shape, BF16) for weight in (*weights, *weights)],
            pltpu.SemaphoreType.DMA((6,)),
        ],
        compiler_params=pltpu.CompilerParams(vmem_limit_bytes=MOST * MIB),
        cost_estimate=pl.CostEstimate(
            flops=20 * slots * width * LANES,
            bytes_accessed=8 * MIB,
            transcendentals=2 * slots * LANES,
        ),
    )(rows[:, PIECE:], own, *weights, *others)

    terms = exchange(partial, QUAD)
    summed = jnp.sum(terms.astype(F32), axis=0).astype(BF16)

    back = exchange(summed.reshape(nodes, HALF, BACK), "z").reshape(slots, BACK)
    chosen = dot(place[:, :slots], back).astype(BF16)
    home = exchange(chosen.reshape(64, BACK // LANES, LANES), LOCAL)
    return pl.pallas_call(
        sum_kernel,
        out_shape=(
            jax.ShapeDtypeStruct((1, width), BF16),
            jax.ShapeDtypeStruct((1, 8), F32),
        ),
        in_specs=[VMEM],
        out_specs=(VMEM, VMEM),
        compiler_params=pltpu.CompilerParams(vmem_limit_bytes=4 * MIB),
    )(home)


def solution(mesh):
    fine = Mesh(mesh.devices.reshape(mesh.devices.shape[0], 4, 2, 4, 2), AXES)
    row = P(AXES, None)
    block = P(AXES, None, None)
    return jax.shard_map(
        on_device,
        mesh=fine,
        in_specs=(row, row, row, row, block, block, block),
        out_specs=(row, row),
        check_vma=False,
    )
```

```python
import jax
import jax.numpy as jnp
from jax import lax
from jax.experimental import pallas as pl
from jax.experimental.pallas import tpu as pltpu
from jax.sharding import Mesh
from jax.sharding import PartitionSpec as P

AXES = ("z", "yh", "yl", "x", "c")
LOCAL = ("yh", "yl", "x", "c")
QUAD = ("x", "yl")
SWAP = ((0, 1), (1, 0))
F32 = jnp.float32
BF16 = jnp.bfloat16
LANES = 128
TILES = 7
PIECE = TILES * LANES
HALF = 4
BACK = 512
NT = (((1,), (1,)), ((), ()))
TN = (((0,), (0,)), ((), ()))
VMEM = pl.BlockSpec(memory_space=pltpu.VMEM)
HBM = pl.BlockSpec(memory_space=pltpu.HBM)
WHOLE = 56
MOST = 51
MIB = 1024 * 1024


def dot(a, b, dims=(((1,), (0,)), ((), ()))):
    return lax.dot_general(a, b, dims, preferred_element_type=F32)


def exchange(value, axes):
    return lax.all_to_all(value, axes, split_axis=0, concat_axis=0, tiled=True)


def quad_of(piece):
    return piece % 4 * 2 + piece // 4


def pack_kernel(x_hbm, dy_hbm, gate_hbm, dest_hbm, out_ref, x_ref, dy_ref, gate_ref, dest_ref, arrived):
    copies = [
        pltpu.make_async_copy(source, target, arrived.at[i])
        for i, (source, target) in enumerate(
            ((x_hbm, x_ref), (dy_hbm, dy_ref), (gate_hbm, gate_ref), (dest_hbm, dest_ref))
        )
    ]
    for copy in copies:
        copy.start()
    for copy in copies:
        copy.wait()
    gate = gate_ref[...].astype(F32)
    dest = dest_ref[...].astype(F32)
    aux = jnp.concatenate([gate, dest, jnp.zeros((1, LANES - 16), F32)], axis=1)
    for q in range(8):
        ref, base = (x_ref, q * PIECE) if q < 4 else (dy_ref, (q - 4) * PIECE)
        rows = [ref[:, base + k * LANES : base + (k + 1) * LANES].astype(F32) for k in range(TILES)]
        tile = jnp.concatenate(rows + [aux], axis=0).astype(BF16)
        for pair in range(4):
            for core in range(2):
                out_ref[pair * 16 + q * 2 + core] = tile


def place_kernel(got_ref, send_ref, place_ref, wide):
    tokens, slots = place_ref.shape
    pair = lax.axis_index("yh")
    core = lax.axis_index("c")
    wide[...] = got_ref[...].astype(F32)
    aux = wide[pl.ds(TILES, tokens, stride=8), :]
    lane = lax.broadcasted_iota(jnp.int32, (tokens, LANES), 1)
    dest = jnp.sum(jnp.where(lane == 8 + 2 * pair, aux, 0.0), axis=1, keepdims=True)
    named = (dest == lane.astype(F32)).astype(F32)
    row = lax.broadcasted_iota(jnp.int32, (tokens, tokens), 0)
    col = lax.broadcasted_iota(jnp.int32, (tokens, tokens), 1)
    earlier = (col < row).astype(F32).astype(BF16)
    before = dot(earlier, named.astype(BF16))
    rank = jnp.sum(before * named, axis=1, keepdims=True)
    slot = lax.broadcasted_iota(jnp.int32, (tokens, slots), 1).astype(F32)
    at = rank - HALF * core.astype(F32)
    code = jnp.where(jnp.logical_and(at >= 0.0, at < HALF), dest * HALF + at, -1.0)
    place = (code == slot).astype(F32).astype(BF16)
    place_ref[...] = place
    for k in range(TILES + 1):
        part = wide[pl.ds(k, tokens, stride=8), :].astype(BF16)
        send_ref[:, k * LANES : (k + 1) * LANES] = dot(place, part, TN).astype(BF16)


def expert_kernel(aux_ref, rows_ref, *refs):
    sources, (out_ref, *weights, arrived) = refs[:6], refs[6:]
    copies = [
        pltpu.make_async_copy(source, target, arrived.at[i])
        for i, (source, target) in enumerate(zip(sources, weights))
    ]
    for copy in copies:
        copy.start()
    column = 2 * lax.axis_index("yh") + lax.axis_index("yl")
    rows = rows_ref.shape[1]
    lane = lax.broadcasted_iota(jnp.int32, (rows, LANES), 1)
    prob = jnp.where(lane == column, aux_ref[...].astype(F32), 0.0)
    prob = jnp.sum(prob, axis=1, keepdims=True)
    x = jnp.concatenate([rows_ref[quad_of(q)] for q in range(4)], axis=1)
    dy = jnp.concatenate([rows_ref[quad_of(q)] for q in range(4, 8)], axis=1)
    gate_terms = jnp.zeros((rows, 1), F32)
    grads = []
    for core in range(2):
        for copy in copies[3 * core : 3 * core + 3]:
            copy.wait()
        gate_w, up_w, down_w = weights[3 * core : 3 * core + 3]
        both = dot(x, jnp.concatenate([gate_w[...], up_w[...]], axis=1))
        gate, up = both[:, :LANES], both[:, LANES:]
        back = dot(dy, down_w[...], NT)
        logistic = jax.nn.sigmoid(gate)
        swished = gate * logistic
        gate_terms += jnp.sum(swished * up * back, axis=1, keepdims=True)
        scaled = prob * back
        slope = scaled * up * logistic * (1.0 + gate * (1.0 - logistic))
        grads += [slope.astype(BF16), (scaled * swished).astype(BF16)]
    grad = jnp.concatenate(grads, axis=1)
    for q in range(7):
        at = slice(q * BACK, (q + 1) * BACK)
        wide = [weights[i][at, :] for i in (0, 1, 3, 4)]
        out_ref[quad_of(q)] = dot(grad, jnp.concatenate(wide, axis=1), NT).astype(BF16)
    lane = lax.broadcasted_iota(jnp.int32, (rows, BACK), 1)
    out_ref[quad_of(7)] = jnp.where(lane == column, gate_terms, 0.0).astype(BF16)


def sum_kernel(home_ref, grad_ref, gate_ref):
    for q in range(8):
        parts = [home_ref[pair * 16 + q * 2 + core].astype(F32) for pair in range(4) for core in range(2)]
        total = sum(parts)
        if q == 7:
            gate_ref[...] = total[:1, :8]
        else:
            for k in range(BACK // LANES):
                at = q * BACK + k * LANES
                grad_ref[:, at : at + LANES] = total[k : k + 1, :].astype(BF16)


def on_device(tokens, out_grad, gate_prob, dest_node, w_gate, w_up, w_down):
    nodes = lax.axis_size("z")
    width = tokens.shape[1]
    slots = nodes * HALF
    weights = (w_gate[0], w_up[0], w_down[0])

    out = pl.pallas_call(
        pack_kernel,
        out_shape=jax.ShapeDtypeStruct((64, 8, LANES), BF16),
        in_specs=[HBM] * 4,
        out_specs=VMEM,
        scratch_shapes=[
            pltpu.VMEM(tokens.shape, BF16),
            pltpu.VMEM(out_grad.shape, BF16),
            pltpu.VMEM(gate_prob.shape, BF16),
            pltpu.VMEM(dest_node.shape, jnp.int32),
            pltpu.SemaphoreType.DMA((4,)),
        ],
        compiler_params=pltpu.CompilerParams(vmem_limit_bytes=WHOLE * MIB),
    )(tokens, out_grad, gate_prob, dest_node)
    got = exchange(out, LOCAL)

    send, place = pl.pallas_call(
        place_kernel,
        out_shape=(
            jax.ShapeDtypeStruct((16 * HALF, PIECE + LANES), BF16),
            jax.ShapeDtypeStruct((64, 16 * HALF), BF16),
        ),
        in_specs=[VMEM],
        out_specs=(VMEM, VMEM),
        scratch_shapes=[pltpu.VMEM((64 * 8, LANES), F32)],
        compiler_params=pltpu.CompilerParams(vmem_limit_bytes=4 * MIB),
    )(got.reshape(64 * 8, LANES))
    rows = exchange(send[:slots].reshape(nodes, HALF, PIECE + LANES), "z")
    rows = rows.reshape(slots, PIECE + LANES)

    others = [lax.ppermute(weight, "c", SWAP) for weight in weights]
    own = exchange(jnp.broadcast_to(rows[None, :, :PIECE], (8, slots, PIECE)), QUAD)
    partial = pl.pallas_call(
        expert_kernel,
        out_shape=jax.ShapeDtypeStruct((8, slots, BACK), BF16),
        in_specs=[VMEM] * 2 + [HBM] * 6,
        out_specs=VMEM,
        scratch_shapes=[
            *[pltpu.VMEM(weight.shape, BF16) for weight in (*weights, *weights)],
            pltpu.SemaphoreType.DMA((6,)),
        ],
        compiler_params=pltpu.CompilerParams(vmem_limit_bytes=MOST * MIB),
        cost_estimate=pl.CostEstimate(
            flops=20 * slots * width * LANES,
            bytes_accessed=8 * MIB,
            transcendentals=2 * slots * LANES,
        ),
    )(rows[:, PIECE:], own, *weights, *others)

    terms = exchange(partial, QUAD)
    summed = jnp.sum(terms.astype(F32), axis=0).astype(BF16)

    back = exchange(summed.reshape(nodes, HALF, BACK), "z").reshape(slots, BACK)
    chosen = dot(place[:, :slots], back).astype(BF16)
    home = exchange(chosen.reshape(64, BACK // LANES, LANES), LOCAL)
    return pl.pallas_call(
        sum_kernel,
        out_shape=(
            jax.ShapeDtypeStruct((1, width), BF16),
            jax.ShapeDtypeStruct((1, 8), F32),
        ),
        in_specs=[VMEM],
        out_specs=(VMEM, VMEM),
        compiler_params=pltpu.CompilerParams(vmem_limit_bytes=4 * MIB),
    )(home)


def solution(mesh):
    fine = Mesh(mesh.devices.reshape(mesh.devices.shape[0], 4, 2, 4, 2), AXES)
    row = P(AXES, None)
    block = P(AXES, None, None)
    return jax.shard_map(
        on_device,
        mesh=fine,
        in_specs=(row, row, row, row, block, block, block),
        out_specs=(row, row),
        check_vma=False,
    )
```

```python
import jax
import jax.numpy as jnp
from jax import lax
from jax.experimental import pallas as pl
from jax.experimental.pallas import tpu as pltpu
from jax.sharding import Mesh
from jax.sharding import PartitionSpec as P

AXES = ("z", "yh", "yl", "x", "c")
LOCAL = ("yh", "yl", "x", "c")
QUAD = ("yl", "x")
SWAP = ((0, 1), (1, 0))
F32 = jnp.float32
BF16 = jnp.bfloat16
LANES = 128
TILES = 7
PIECE = TILES * LANES
HALF = 4
BACK = 512
NT = (((1,), (1,)), ((), ()))
TN = (((0,), (0,)), ((), ()))
VMEM = pl.BlockSpec(memory_space=pltpu.VMEM)
HBM = pl.BlockSpec(memory_space=pltpu.HBM)
WHOLE = 56
MOST = 51
MIB = 1024 * 1024


def dot(a, b, dims=(((1,), (0,)), ((), ()))):
    return lax.dot_general(a, b, dims, preferred_element_type=F32)


def exchange(value, axes):
    return lax.all_to_all(value, axes, split_axis=0, concat_axis=0, tiled=True)


def pack_kernel(x_hbm, dy_hbm, gate_hbm, dest_hbm, out_ref, x_ref, dy_ref, gate_ref, dest_ref, arrived):
    copies = [
        pltpu.make_async_copy(source, target, arrived.at[i])
        for i, (source, target) in enumerate(
            ((x_hbm, x_ref), (dy_hbm, dy_ref), (gate_hbm, gate_ref), (dest_hbm, dest_ref))
        )
    ]
    for copy in copies:
        copy.start()
    for copy in copies:
        copy.wait()
    gate = gate_ref[...].astype(F32)
    dest = dest_ref[...].astype(F32)
    aux = jnp.concatenate([gate, dest, jnp.zeros((1, LANES - 16), F32)], axis=1)
    for q in range(8):
        ref, base = (x_ref, q * PIECE) if q < 4 else (dy_ref, (q - 4) * PIECE)
        rows = [ref[:, base + k * LANES : base + (k + 1) * LANES].astype(F32) for k in range(TILES)]
        tile = jnp.concatenate(rows + [aux], axis=0).astype(BF16)
        for pair in range(4):
            for core in range(2):
                out_ref[pair * 16 + q * 2 + core] = tile


def place_kernel(got_ref, send_ref, place_ref, wide):
    tokens, slots = place_ref.shape
    pair = lax.axis_index("yh")
    core = lax.axis_index("c")
    wide[...] = got_ref[...].astype(F32)
    aux = wide[pl.ds(TILES, tokens, stride=8), :]
    lane = lax.broadcasted_iota(jnp.int32, (tokens, LANES), 1)
    dest = jnp.sum(jnp.where(lane == 8 + 2 * pair, aux, 0.0), axis=1, keepdims=True)
    named = (dest == lane.astype(F32)).astype(F32)
    row = lax.broadcasted_iota(jnp.int32, (tokens, tokens), 0)
    col = lax.broadcasted_iota(jnp.int32, (tokens, tokens), 1)
    earlier = (col < row).astype(F32).astype(BF16)
    before = dot(earlier, named.astype(BF16))
    rank = jnp.sum(before * named, axis=1, keepdims=True)
    slot = lax.broadcasted_iota(jnp.int32, (tokens, slots), 1).astype(F32)
    at = rank - HALF * core.astype(F32)
    code = jnp.where(jnp.logical_and(at >= 0.0, at < HALF), dest * HALF + at, -1.0)
    place = (code == slot).astype(F32).astype(BF16)
    place_ref[...] = place
    for k in range(TILES + 1):
        part = wide[pl.ds(k, tokens, stride=8), :].astype(BF16)
        send_ref[:, k * LANES : (k + 1) * LANES] = dot(place, part, TN).astype(BF16)


def spread_kernel(rows_ref, out_ref, aux_ref, arrived):
    copies = [
        pltpu.make_async_copy(rows_ref.at[:, :PIECE], out_ref.at[i], arrived.at[i]) for i in range(8)
    ]
    for copy in copies:
        copy.start()
    aux_ref[...] = rows_ref[:, PIECE:]
    for copy in copies:
        copy.wait()


def expert_kernel(aux_ref, rows_ref, *refs):
    sources, (out_ref, *weights, arrived) = refs[:6], refs[6:]
    copies = [
        pltpu.make_async_copy(source, target, arrived.at[i])
        for i, (source, target) in enumerate(zip(sources, weights))
    ]
    for copy in copies:
        copy.start()
    column = 2 * lax.axis_index("yh") + lax.axis_index("yl")
    rows = rows_ref.shape[1]
    lane = lax.broadcasted_iota(jnp.int32, (rows, LANES), 1)
    prob = jnp.where(lane == column, aux_ref[...].astype(F32), 0.0)
    prob = jnp.sum(prob, axis=1, keepdims=True)
    x = jnp.concatenate([rows_ref[i] for i in range(4)], axis=1)
    dy = jnp.concatenate([rows_ref[i] for i in range(4, 8)], axis=1)
    gate_terms = jnp.zeros((rows, 1), F32)
    grads = []
    for core in range(2):
        for copy in copies[3 * core : 3 * core + 3]:
            copy.wait()
        gate_w, up_w, down_w = weights[3 * core : 3 * core + 3]
        both = dot(x, jnp.concatenate([gate_w[...], up_w[...]], axis=1))
        gate, up = both[:, :LANES], both[:, LANES:]
        back = dot(dy, down_w[...], NT)
        logistic = jax.nn.sigmoid(gate)
        swished = gate * logistic
        gate_terms += jnp.sum(swished * up * back, axis=1, keepdims=True)
        scaled = prob * back
        slope = scaled * up * logistic * (1.0 + gate * (1.0 - logistic))
        grads += [slope.astype(BF16), (scaled * swished).astype(BF16)]
    grad = jnp.concatenate(grads, axis=1)
    for q in range(7):
        at = slice(q * BACK, (q + 1) * BACK)
        wide = [weights[i][at, :] for i in (0, 1, 3, 4)]
        out_ref[q] = dot(grad, jnp.concatenate(wide, axis=1), NT).astype(BF16)
    lane = lax.broadcasted_iota(jnp.int32, (rows, BACK), 1)
    out_ref[7] = jnp.where(lane == column, gate_terms, 0.0).astype(BF16)


def sum_kernel(home_ref, grad_ref, gate_ref):
    for q in range(8):
        parts = [home_ref[pair * 16 + q * 2 + core].astype(F32) for pair in range(4) for core in range(2)]
        total = sum(parts)
        if q == 7:
            gate_ref[...] = total[:1, :8]
        else:
            for k in range(BACK // LANES):
                at = q * BACK + k * LANES
                grad_ref[:, at : at + LANES] = total[k : k + 1, :].astype(BF16)


def on_device(tokens, out_grad, gate_prob, dest_node, w_gate, w_up, w_down):
    nodes = lax.axis_size("z")
    width = tokens.shape[1]
    slots = nodes * HALF
    weights = (w_gate[0], w_up[0], w_down[0])

    out = pl.pallas_call(
        pack_kernel,
        out_shape=jax.ShapeDtypeStruct((64, 8, LANES), BF16),
        in_specs=[HBM] * 4,
        out_specs=VMEM,
        scratch_shapes=[
            pltpu.VMEM(tokens.shape, BF16),
            pltpu.VMEM(out_grad.shape, BF16),
            pltpu.VMEM(gate_prob.shape, BF16),
            pltpu.VMEM(dest_node.shape, jnp.int32),
            pltpu.SemaphoreType.DMA((4,)),
        ],
        compiler_params=pltpu.CompilerParams(vmem_limit_bytes=WHOLE * MIB),
    )(tokens, out_grad, gate_prob, dest_node)
    got = exchange(out, LOCAL)

    send, place = pl.pallas_call(
        place_kernel,
        out_shape=(
            jax.ShapeDtypeStruct((16 * HALF, PIECE + LANES), BF16),
            jax.ShapeDtypeStruct((64, 16 * HALF), BF16),
        ),
        in_specs=[VMEM],
        out_specs=(VMEM, VMEM),
        scratch_shapes=[pltpu.VMEM((64 * 8, LANES), F32)],
        compiler_params=pltpu.CompilerParams(vmem_limit_bytes=4 * MIB),
    )(got.reshape(64 * 8, LANES))
    rows = exchange(send[:slots].reshape(nodes, HALF, PIECE + LANES), "z")
    rows = rows.reshape(slots, PIECE + LANES)

    others = [lax.ppermute(weight, "c", SWAP) for weight in weights]
    spread, aux = pl.pallas_call(
        spread_kernel,
        out_shape=(
            jax.ShapeDtypeStruct((8, slots, PIECE), BF16),
            jax.ShapeDtypeStruct((slots, LANES), BF16),
        ),
        in_specs=[VMEM],
        out_specs=(HBM, VMEM),
        scratch_shapes=[pltpu.SemaphoreType.DMA((8,))],
        compiler_params=pltpu.CompilerParams(vmem_limit_bytes=4 * MIB),
    )(rows)
    own = exchange(spread, QUAD)
    partial = pl.pallas_call(
        expert_kernel,
        out_shape=jax.ShapeDtypeStruct((8, slots, BACK), BF16),
        in_specs=[VMEM] * 2 + [HBM] * 6,
        out_specs=VMEM,
        scratch_shapes=[
            *[pltpu.VMEM(weight.shape, BF16) for weight in (*weights, *weights)],
            pltpu.SemaphoreType.DMA((6,)),
        ],
        compiler_params=pltpu.CompilerParams(vmem_limit_bytes=MOST * MIB),
        cost_estimate=pl.CostEstimate(
            flops=20 * slots * width * LANES,
            bytes_accessed=8 * MIB,
            transcendentals=2 * slots * LANES,
        ),
    )(aux, own, *weights, *others)

    terms = exchange(partial, QUAD)
    summed = jnp.sum(terms.astype(F32), axis=0).astype(BF16)

    back = exchange(summed.reshape(nodes, HALF, BACK), "z").reshape(slots, BACK)
    chosen = dot(place[:, :slots], back).astype(BF16)
    home = exchange(chosen.reshape(64, BACK // LANES, LANES), LOCAL)
    return pl.pallas_call(
        sum_kernel,
        out_shape=(
            jax.ShapeDtypeStruct((1, width), BF16),
            jax.ShapeDtypeStruct((1, 8), F32),
        ),
        in_specs=[VMEM],
        out_specs=(VMEM, VMEM),
        compiler_params=pltpu.CompilerParams(vmem_limit_bytes=4 * MIB),
    )(home)


def solution(mesh):
    fine = Mesh(mesh.devices.reshape(mesh.devices.shape[0], 4, 2, 4, 2), AXES)
    row = P(AXES, None)
    block = P(AXES, None, None)
    return jax.shard_map(
        on_device,
        mesh=fine,
        in_specs=(row, row, row, row, block, block, block),
        out_specs=(row, row),
        check_vma=False,
    )
```
